32 devices in a mesh: groups: 2 (over x), space: 16 (over z, y, core).
Axes of the slice: x: 2, y: 2, z: 4, core: 2. Of those that a mesh axis runs over, the one named last changes fastest.
Arguments:
- prior_states: bfloat16 [2, 128, 8, 65536], P(None, None, None, ('groups', 'space')), parts along dimension 3, may hold values from -6 to 6
- mixing_matrix: bfloat16 [128, 256], P(None, 'groups'), parts along dimension 1, may hold values from -0.5 to 0.5
- capacity_factor: bfloat16 [8, 65536], P(None, ('groups', 'space')), parts along dimension 1, may hold values from 0.5 to 4
- live_flags: int32 [8, 65536], P(None, ('groups', 'space')), parts along dimension 1, may hold values 0 or 1
- borehole_block_location: int32 [8, 64], P(None, 'groups'), parts along dimension 1, may hold values from 0 to 32767
- borehole_injection_speed: float32 [8, 64], P(None, 'groups'), parts along dimension 1, may hold values from -8 to 8
Outputs:
- pressure: float32 [2048, 16, 8, 256], P(('groups', 'space')), parts along dimension 0
The draws below stay inside these ranges and needn't reach their ends.
There are 2 independent parts, one for each index of `groups`. The reference program is written for one: setup_inputs(seed, part) draws one part's arguments, and reference() takes and returns one part's arrays. A program takes and returns all parts, laid end to end along the dimension named above; each array names one. Nothing has to cross between parts.
All inputs are finite; a program needn't handle non-finite values. No bound on the sum of `live_flags` on one device may be relied on, other than what follows from the above.
Results may differ from the reference program's by a relative error of at most 0.004.
Values may be sent and summed in bfloat16 or wider, within the bound.
A program may use at most 256 MiB of HBM per device.

```python
import math
import jax
import jax.numpy as jnp
from jax import lax

REALIZATIONS = 128
SLAB_BLOCKS = 8
TX = 16
NZ = 8
NY = 256
SWEEPS = 3
WELLS = 32
BLOCK_VOLUMES = 32768


def plant(drawn, key, least, top_value):
    longest = drawn.shape.index(max(drawn.shape))
    spots = []
    for shift in (0, 1):
        where = [jax.random.randint(jax.random.fold_in(key, axis), (), 0, length) for axis, length in enumerate(drawn.shape)]
        where[longest] = (where[longest] + shift) % drawn.shape[longest]
        spots.append(tuple(where))
    return drawn.at[spots[0]].set(least).at[spots[1]].set(top_value)


def shard_levels(stream_key, shape, shards, least, largest):
    factor_of = 1.0
    for axis_at, blocks in shards:
        heights = jax.random.uniform(jax.random.fold_in(jax.random.fold_in(stream_key, 6), axis_at), (blocks,), jnp.float32, least / len(shards), largest / len(shards))
        factor_of = factor_of * jnp.repeat(jnp.exp(heights), shape[axis_at] // blocks).reshape((-1,) + (1,) * (len(shape) - 1 - axis_at))
    return factor_of


def centred(stream_key, extent, deviation, bound, pieces=(), kind=jnp.bfloat16):
    drawn = deviation * jax.random.normal(stream_key, extent, jnp.float32)
    if pieces:
        drawn = drawn * shard_levels(stream_key, extent, pieces, -0.22, 0.18)
    return jnp.clip(drawn, -bound, bound).astype(kind)


def setup_inputs(seed: int = 0, part: int = 0) -> dict:
    seeds = jax.random.split(jax.random.key(seed), 7)
    part_splits = jax.random.split(jax.random.fold_in(seeds[6], part), 7)
    prior_states = centred(part_splits[0], (2, REALIZATIONS, SLAB_BLOCKS, BLOCK_VOLUMES), 1.0, 6.0, ((3, 16),))
    mixing_matrix = centred(part_splits[1], (REALIZATIONS, REALIZATIONS), REALIZATIONS ** -0.5, 0.5)
    capacity_factor = jnp.clip(jnp.exp(math.log(4.0) - 2.0794415 * jax.random.uniform(part_splits[2], (SLAB_BLOCKS, BLOCK_VOLUMES), jnp.float32) ** shard_levels(part_splits[2], (SLAB_BLOCKS, BLOCK_VOLUMES), ((1, 16),), -0.2, 0.2)), 0.5, 4.0).astype(jnp.bfloat16)
    live_flags = plant((jax.random.randint(part_splits[3], (SLAB_BLOCKS, BLOCK_VOLUMES), 0, 8) < 7).astype(jnp.int32), jax.random.fold_in(part_splits[3], 1), 0, 1)
    borehole_block_location = plant(jax.random.randint(part_splits[4], (SLAB_BLOCKS, WELLS), 0, BLOCK_VOLUMES), jax.random.fold_in(part_splits[4], 1), 0, BLOCK_VOLUMES - 1).astype(jnp.int32)
    borehole_injection_speed = centred(part_splits[5], (SLAB_BLOCKS, WELLS), 3.0, 8.0, (), jnp.float32)
    return dict(prior_states=prior_states, mixing_matrix=mixing_matrix, capacity_factor=capacity_factor, live_flags=live_flags, borehole_block_location=borehole_block_location, borehole_injection_speed=borehole_injection_speed)


def mobility(value):
    return 1.0 / (1.0 + 0.25 * value * value)


def neighbours(padded):
    return (padded[..., 2:, 1:-1, 1:-1], padded[..., :-2, 1:-1, 1:-1],
            padded[..., 1:-1, 2:, 1:-1], padded[..., 1:-1, :-2, 1:-1],
            padded[..., 1:-1, 1:-1, 2:], padded[..., 1:-1, 1:-1, :-2])


def combine(press_pad, flow_pad, storage_tile, start_field, source):
    flow_mid = flow_pad[..., 1:-1, 1:-1, 1:-1]
    numerator = storage_tile * start_field + source
    denominator = storage_tile
    for nb_press, nb_flow in zip(neighbours(press_pad), neighbours(flow_pad)):
        face_term = 0.5 * (flow_mid + nb_flow)
        numerator = numerator + face_term * nb_press
        denominator = denominator + face_term
    return numerator / denominator


def reference(prior_states, mixing_matrix, capacity_factor, live_flags, borehole_block_location, borehole_injection_speed):
    grid_volume_number = SLAB_BLOCKS * TX * NZ * NY
    grid_shape = (SLAB_BLOCKS * TX, NZ, NY)
    conductivity_lines = prior_states[0].reshape(REALIZATIONS, grid_volume_number)
    head_lines = prior_states[1].reshape(REALIZATIONS, grid_volume_number)
    mixed_logs = jnp.dot(mixing_matrix.T, conductivity_lines, preferred_element_type=jnp.float32).astype(jnp.bfloat16)
    mixed_press = jnp.dot(mixing_matrix.T, head_lines, preferred_element_type=jnp.float32).astype(jnp.bfloat16)
    storage_tile = capacity_factor.astype(jnp.float32).reshape(grid_shape)
    active_mask = live_flags.astype(jnp.float32).reshape(grid_volume_number)
    offsets = (jnp.arange(SLAB_BLOCKS, dtype=jnp.int32) * (TX * NZ * NY))[:, None]
    source = jnp.zeros((grid_volume_number,), jnp.float32).at[(borehole_block_location + offsets).reshape(-1)].add(
        borehole_injection_speed.reshape(-1)).reshape(grid_shape)

    def member(rows):
        log_perm, start_bf = rows
        log_perm = lax.optimization_barrier(log_perm)
        perm_bf = (active_mask * jnp.exp(log_perm.astype(jnp.float32))).astype(jnp.bfloat16)
        perm_bf = lax.optimization_barrier(perm_bf)
        perm_field = perm_bf.astype(jnp.float32).reshape(grid_shape)
        start_bf = lax.optimization_barrier(start_bf)
        start_field = start_bf.astype(jnp.float32).reshape(grid_shape)
        pressure = start_field
        for sweep_index in range(SWEEPS):
            press_pad = jnp.pad(pressure, 1)
            flow_pad = jnp.pad(perm_field * mobility(pressure), 1)
            pressure = combine(press_pad, flow_pad, storage_tile, start_field, source)
        return pressure

    result = lax.map(member, (mixed_logs, mixed_press))
    result = result.reshape(REALIZATIONS, SLAB_BLOCKS, TX, NZ, NY).transpose(1, 0, 2, 3, 4)
    return result.reshape(SLAB_BLOCKS * REALIZATIONS, TX, NZ, NY)
```

```python
import functools

import jax
import jax.numpy as jnp
from jax import lax
from jax.experimental import pallas as pl
from jax.experimental.pallas import tpu as pltpu
from jax.sharding import PartitionSpec as P

SLAB_BLOCKS = 8
TX = 16
NZ = 8
NY = 256
SWEEPS = 3
PLANE = NZ * NY
HALO = SWEEPS
PADDED = TX + 2 * HALO
CHUNK = 8
MESH = pl.DeviceIdType.MESH


def kernel(
    space,
    members,
    piece,
    depth,
    prior_ref,
    mix_ref,
    cap_ref,
    live_ref,
    where_ref,
    speed_ref,
    out_ref,
    weights,
    states,
    send,
    recv,
    result,
    press,
    flow,
    carried,
    storage,
    source,
    source_rows,
    cap_send,
    cap_recv,
    state_sem,
    send_sem,
    recv_sem,
    halo_send_sem,
    halo_recv_sem,
    cap_send_sem,
    cap_recv_sem,
    edge_send_sem,
    edge_recv_sem,
    out_sem,
):
    groups = space // SLAB_BLOCKS
    share = members // groups
    chunks = share // CHUNK
    rows_z = piece // NY
    per_plane = PLANE // piece
    pieces = TX * per_plane
    edge = HALO * per_plane

    me = lax.axis_index("space")
    tile = me // groups
    wells = where_ref.shape[1]

    barrier = pltpu.get_barrier_semaphore()

    @pl.loop(1, space)
    def _(d):
        pl.semaphore_signal(
            barrier, inc=1, device_id={"space": lax.rem(me + d, space)}, device_id_type=MESH
        )

    def state_copy(i):
        t = lax.rem(tile + SLAB_BLOCKS // 2 + i, SLAB_BLOCKS)
        slot = lax.rem(i, 2)
        return pltpu.make_async_copy(prior_ref.at[t], states.at[slot], state_sem.at[slot])

    state_copy(0).start()
    weights[...] = mix_ref[...].astype(jnp.float32).T.astype(jnp.bfloat16)
    caps = cap_ref[...].astype(jnp.float32)
    for t in range(SLAB_BLOCKS):
        cap_send[t] = caps[t : t + 1, :]

    @pl.when(tile == 0)
    def _():
        @pl.loop(0, chunks)
        def _(c):
            for j in range(edge):
                recv[c, j] = jnp.zeros_like(recv[c, j])

        for b in range(2):
            for j in range(HALO):
                for ref in (press, flow, carried):
                    ref[b, j] = jnp.zeros_like(ref[b, j])

    @pl.when(tile == SLAB_BLOCKS - 1)
    def _():
        @pl.loop(0, chunks)
        def _(c):
            for j in range(edge):
                recv[c, edge + pieces + j] = jnp.zeros_like(recv[c, j])

        for b in range(2):
            for j in range(HALO):
                for ref in (press, flow, carried):
                    ref[b, HALO + TX + j] = jnp.zeros_like(ref[b, j])

    pl.semaphore_wait(barrier, space - 1)

    def send_piece(c, dest):
        @pl.when(dest != me)
        def _():
            pltpu.make_async_remote_copy(
                src_ref=send.at[c, dest],
                dst_ref=recv.at[c, edge + me],
                send_sem=send_sem.at[c],
                recv_sem=recv_sem.at[c],
                device_id={"space": dest},
                device_id_type=MESH,
            ).start()

        @pl.when(dest == me)
        def _():
            pltpu.make_async_copy(
                send.at[c, dest], recv.at[c, edge + me], recv_sem.at[c]
            ).start()

    def send_chunk(c):
        @pl.loop(0, space)
        def _(d):
            send_piece(c, lax.rem(me + space // 2 + d, space))

    @pl.loop(0, space)
    def _(d):
        dest = lax.rem(me + d, space)

        @pl.when(dest != me)
        def _():
            pltpu.make_async_remote_copy(
                src_ref=cap_send.at[dest // groups],
                dst_ref=cap_recv.at[edge + me],
                send_sem=cap_send_sem,
                recv_sem=cap_recv_sem,
                device_id={"space": dest},
                device_id_type=MESH,
            ).start()

        @pl.when(dest == me)
        def _():
            pltpu.make_async_copy(
                cap_send.at[dest // groups], cap_recv.at[edge + me], cap_recv_sem
            ).start()

    def edges(buffer, send_sems, recv_sems):
        up = pltpu.make_async_remote_copy(
            src_ref=buffer.at[pl.ds(pieces, edge)],
            dst_ref=buffer.at[pl.ds(0, edge)],
            send_sem=send_sems.at[0],
            recv_sem=recv_sems.at[0],
            device_id={"space": lax.rem(me + groups, space)},
            device_id_type=MESH,
        )
        down = pltpu.make_async_remote_copy(
            src_ref=buffer.at[pl.ds(edge, edge)],
            dst_ref=buffer.at[pl.ds(edge + pieces, edge)],
            send_sem=send_sems.at[1],
            recv_sem=recv_sems.at[1],
            device_id={"space": lax.rem(me + space - groups, space)},
            device_id_type=MESH,
        )
        return up, down

    def start_edges(*args):
        up, down = edges(*args)

        @pl.when(tile < SLAB_BLOCKS - 1)
        def _():
            up.start()

        @pl.when(tile > 0)
        def _():
            down.start()

    def wait_edges(*args):
        up, down = edges(*args)

        @pl.when(tile > 0)
        def _():
            up.wait_recv()

        @pl.when(tile < SLAB_BLOCKS - 1)
        def _():
            down.wait_recv()

    def wait_edges_sent(*args):
        up, down = edges(*args)

        @pl.when(tile < SLAB_BLOCKS - 1)
        def _():
            up.wait_send()

        @pl.when(tile > 0)
        def _():
            down.wait_send()

    cap_edges = (cap_recv, edge_send_sem, edge_recv_sem)

    @pl.loop(0, SLAB_BLOCKS)
    def _(i):
        t = lax.rem(tile + SLAB_BLOCKS // 2 + i, SLAB_BLOCKS)
        slot = lax.rem(i, 2)

        @pl.when(i + 1 < SLAB_BLOCKS)
        def _():
            state_copy(i + 1).start()

        state_copy(i).wait()
        for j in range(rows_z):
            lanes = pl.ds(j * NY, NY)
            logs = jnp.dot(
                weights[...], states[slot, 0, :, lanes], preferred_element_type=jnp.float32
            )
            start = jnp.dot(
                weights[...], states[slot, 1, :, lanes], preferred_element_type=jnp.float32
            )
            live = live_ref[pl.ds(t, 1), lanes].astype(jnp.float32)
            perm = live * jnp.exp(logs.astype(jnp.bfloat16).astype(jnp.float32))
            for v in range(groups):
                for c in range(chunks):
                    r = v * share + c * CHUNK
                    both = jnp.concatenate([perm[r : r + CHUNK], start[r : r + CHUNK]], axis=0)
                    send[c, t * groups + v, :, lanes] = both.astype(jnp.bfloat16)

        @pl.loop(0, groups)
        def _(v):
            send_piece(0, t * groups + v)

        @pl.when(i == 2)
        def _():
            pltpu.make_async_copy(
                cap_recv.at[pl.ds(edge, pieces)], cap_recv.at[pl.ds(edge, pieces)], cap_recv_sem
            ).wait()
            start_edges(*cap_edges)

    @pl.loop(1, min(depth, chunks))
    def _(c):
        send_chunk(c)

    source_rows[...] = jnp.zeros_like(source_rows)
    cell = lax.broadcasted_iota(jnp.int32, source_rows.shape, 0) * PLANE
    cell = cell + lax.broadcasted_iota(jnp.int32, source_rows.shape, 1)

    @pl.loop(0, wells)
    def _(w):
        for shift in (-1, 0, 1):
            t = jnp.clip(tile + shift, 0, SLAB_BLOCKS - 1)
            spot = where_ref[t, w] + (HALO + shift * TX) * PLANE
            rate = speed_ref[t, w] * (1.0 / 16.0)
            source_rows[...] += jnp.where(cell == spot, rate, 0.0)

    wait_edges(*cap_edges)

    for x in range(PADDED):
        for z in range(NZ):
            held = cap_recv[
                x * per_plane + z // rows_z, :, (z % rows_z) * NY : (z % rows_z + 1) * NY
            ]
            storage[x, z] = jnp.broadcast_to(held * (1.0 / 16.0), (CHUNK, NY))
            source[x, z] = jnp.broadcast_to(
                source_rows[x : x + 1, z * NY : (z + 1) * NY], (CHUNK, NY)
            )

    lane = lax.broadcasted_iota(jnp.int32, (CHUNK, NY), 1)
    first, last = lane == 0, lane == NY - 1

    def fields(c, x, z):
        both = recv[
            c, x * per_plane + z // rows_z, :, pl.ds((z % rows_z) * NY, NY)
        ].astype(jnp.float32)
        return both[:CHUNK], both[CHUNK:]

    def keep(b, x, z, p, perm):
        h = perm / (32.0 + 8.0 * p * p)
        press[b, x, z] = p
        flow[b, x, z] = h
        carried[b, x, z] = h * p

    def updated(b, x, z, start):
        p, h = press[b, x, z], flow[b, x, z]
        sides = [(x - 1, z), (x + 1, z)]
        if z > 0:
            sides.append((x, z - 1))
        if z < NZ - 1:
            sides.append((x, z + 1))
        p_left = jnp.where(first, 0.0, pltpu.roll(p, 1, 1))
        h_left = jnp.where(first, 0.0, pltpu.roll(h, 1, 1))
        p_right = jnp.where(last, 0.0, pltpu.roll(p, NY - 1, 1))
        h_right = jnp.where(last, 0.0, pltpu.roll(h, NY - 1, 1))
        p_sum = p_left + p_right
        h_sum = h_left + h_right
        hp_sum = h_left * p_left + h_right * p_right
        for at in sides:
            p_sum = p_sum + press[(b,) + at]
            h_sum = h_sum + flow[(b,) + at]
            hp_sum = hp_sum + carried[(b,) + at]
        s = storage[x, z]
        above = s * start + source[x, z] + h * p_sum + hp_sum
        below = s + 6.0 * h + h_sum
        return above / below

    def relax(c):
        @pl.loop(0, PADDED)
        def _(x):
            for z in range(NZ):
                perm, start = fields(c, x, z)
                keep(0, x, z, start, perm)

        for sweep in range(SWEEPS):
            b = sweep % 2
            reach = SWEEPS - 1 - sweep
            low = HALO - jnp.where(tile == 0, 0, reach)
            high = HALO + TX + jnp.where(tile == SLAB_BLOCKS - 1, 0, reach)

            def plane(x, _, b=b, sweep=sweep):
                for z in range(NZ):
                    perm, start = fields(c, x, z)
                    p = updated(b, x, z, start)
                    if sweep < SWEEPS - 1:
                        keep(1 - b, x, z, p, perm)
                    else:
                        result[c, x - HALO, z] = p
                return 0

            lax.fori_loop(low, high, plane, 0)

    def out_copy(c):
        return pltpu.make_async_copy(
            result.at[c], out_ref.at[:, :, pl.ds(c * CHUNK, CHUNK), :], out_sem.at[c]
        )

    def halo(c):
        return recv.at[c], halo_send_sem.at[c], halo_recv_sem.at[c]

    @pl.loop(0, chunks + 1)
    def _(c):
        @pl.when(c < chunks)
        def _():
            got = recv.at[c, pl.ds(edge, pieces)]
            pltpu.make_async_copy(got, got, recv_sem.at[c]).wait()
            start_edges(*halo(c))

        @pl.when(c + depth < chunks)
        def _():
            send_chunk(c + depth)

        @pl.when(c > 0)
        def _():
            wait_edges(*halo(c - 1))
            relax(c - 1)
            out_copy(c - 1).start()

    @pl.loop(0, chunks)
    def _(c):
        sent = send.at[c, pl.ds(0, space - 1)]
        pltpu.make_async_copy(sent, sent, send_sem.at[c]).wait()
        wait_edges_sent(*halo(c))
        out_copy(c).wait()

    sent = cap_recv.at[pl.ds(0, space - 1)]
    pltpu.make_async_copy(sent, sent, cap_send_sem).wait()
    wait_edges_sent(*cap_edges)


def on_device(
    prior_states,
    mixing_matrix,
    capacity_factor,
    live_flags,
    borehole_block_location,
    borehole_injection_speed,
):
    space = lax.axis_size("space")
    groups = space // SLAB_BLOCKS
    members = mixing_matrix.shape[0]
    share = members // groups
    chunks = share // CHUNK
    piece = prior_states.shape[3]
    per_plane = PLANE // piece
    padded_pieces = PADDED * per_plane
    by_tile = prior_states.transpose(2, 0, 1, 3)
    vmem = pl.BlockSpec(memory_space=pltpu.VMEM)
    smem = pl.BlockSpec(memory_space=pltpu.SMEM)
    hbm = pl.BlockSpec(memory_space=pl.ANY)
    dma = pltpu.SemaphoreType.DMA
    slab = (PADDED, NZ, CHUNK, NY)
    out = pl.pallas_call(
        functools.partial(kernel, space, members, piece, 2),
        out_shape=jax.ShapeDtypeStruct((TX, NZ, share, NY), jnp.float32),
        in_specs=[hbm, vmem, vmem, vmem, smem, smem],
        out_specs=hbm,
        scratch_shapes=[
            pltpu.VMEM((members, members), jnp.bfloat16),
            pltpu.VMEM((2, 2, members, piece), jnp.bfloat16),
            pltpu.VMEM((chunks, space, 2 * CHUNK, piece), jnp.bfloat16),
            pltpu.VMEM((chunks, padded_pieces, 2 * CHUNK, piece), jnp.bfloat16),
            pltpu.VMEM((chunks, TX, NZ, CHUNK, NY), jnp.float32),
            pltpu.VMEM((2,) + slab, jnp.float32),
            pltpu.VMEM((2,) + slab, jnp.float32),
            pltpu.VMEM((2,) + slab, jnp.float32),
            pltpu.VMEM(slab, jnp.float32),
            pltpu.VMEM(slab, jnp.float32),
            pltpu.VMEM((-(-PADDED // 8) * 8, PLANE), jnp.float32),
            pltpu.VMEM((SLAB_BLOCKS, 1, piece), jnp.float32),
            pltpu.VMEM((padded_pieces, 1, piece), jnp.float32),
            dma((2,)),
            dma((chunks,)),
            dma((chunks,)),
            dma((chunks, 2)),
            dma((chunks, 2)),
            dma(()),
            dma(()),
            dma((2,)),
            dma((2,)),
            dma((chunks,)),
        ],
        compiler_params=pltpu.CompilerParams(
            collective_id=0, has_side_effects=True, vmem_limit_bytes=56 * 1024 * 1024
        ),
    )(
        by_tile,
        mixing_matrix,
        capacity_factor,
        live_flags,
        borehole_block_location,
        borehole_injection_speed,
    )
    return out.transpose(2, 0, 1, 3)


def solution(mesh):
    placed = (
        P(None, None, None, ("groups", "space")),
        P(None, "groups"),
        P(None, ("groups", "space")),
        P(None, ("groups", "space")),
        P(None, "groups"),
        P(None, "groups"),
    )
    return jax.shard_map(
        on_device,
        mesh=mesh,
        in_specs=placed,
        out_specs=P(("groups", "space"), None, None, None),
        check_vma=False,
    )
```

```python
import functools

import jax
import jax.numpy as jnp
from jax import lax
from jax.experimental import pallas as pl
from jax.experimental.pallas import tpu as pltpu
from jax.sharding import PartitionSpec as P

SLAB_BLOCKS = 8
TX = 16
NZ = 8
NY = 256
SWEEPS = 3
PLANE = NZ * NY
HALO = SWEEPS
PADDED = TX + 2 * HALO
CHUNK = 8
MESH = pl.DeviceIdType.MESH


def turn(mine, i, count):
    half = count // 2
    here = mine // half
    side = lax.rem(here + i + 1, 2)
    return side * half + lax.rem(mine + i // 2, half)


def kernel(
    space,
    members,
    piece,
    depth,
    prior_ref,
    mix_ref,
    cap_ref,
    live_ref,
    where_ref,
    speed_ref,
    out_ref,
    weights,
    states,
    send,
    recv,
    result,
    press,
    flow,
    carried,
    storage,
    source,
    source_rows,
    cap_send,
    cap_recv,
    state_sem,
    send_sem,
    recv_sem,
    halo_send_sem,
    halo_recv_sem,
    cap_send_sem,
    cap_recv_sem,
    edge_send_sem,
    edge_recv_sem,
    out_sem,
    middle_sem,
):
    groups = space // SLAB_BLOCKS
    share = members // groups
    chunks = share // CHUNK
    rows_z = piece // NY
    per_plane = PLANE // piece
    pieces = TX * per_plane
    edge = HALO * per_plane

    me = lax.axis_index("space")
    tile = me // groups
    wells = where_ref.shape[1]

    barrier = pltpu.get_barrier_semaphore()

    @pl.loop(1, space)
    def _(d):
        pl.semaphore_signal(
            barrier, inc=1, device_id={"space": lax.rem(me + d, space)}, device_id_type=MESH
        )

    def state_copy(i):
        t = turn(tile, i, SLAB_BLOCKS)
        slot = lax.rem(i, 2)
        return pltpu.make_async_copy(prior_ref.at[t], states.at[slot], state_sem.at[slot])

    state_copy(0).start()
    weights[...] = mix_ref[...].astype(jnp.float32).T.astype(jnp.bfloat16)
    caps = cap_ref[...].astype(jnp.float32)
    for t in range(SLAB_BLOCKS):
        cap_send[t] = caps[t : t + 1, :]

    @pl.when(tile == 0)
    def _():
        @pl.loop(0, chunks)
        def _(c):
            for j in range(edge):
                recv[c, j] = jnp.zeros_like(recv[c, j])

        for b in range(2):
            for j in range(HALO):
                for ref in (press, flow, carried):
                    ref[b, j] = jnp.zeros_like(ref[b, j])

    @pl.when(tile == SLAB_BLOCKS - 1)
    def _():
        @pl.loop(0, chunks)
        def _(c):
            for j in range(edge):
                recv[c, edge + pieces + j] = jnp.zeros_like(recv[c, j])

        for b in range(2):
            for j in range(HALO):
                for ref in (press, flow, carried):
                    ref[b, HALO + TX + j] = jnp.zeros_like(ref[b, j])

    pl.semaphore_wait(barrier, space - 1)

    def send_piece(c, dest):
        @pl.when(dest != me)
        def _():
            pltpu.make_async_remote_copy(
                src_ref=send.at[c, dest],
                dst_ref=recv.at[c, edge + me],
                send_sem=send_sem.at[c],
                recv_sem=recv_sem.at[c],
                device_id={"space": dest},
                device_id_type=MESH,
            ).start()

        @pl.when(dest == me)
        def _():
            pltpu.make_async_copy(
                send.at[c, dest], recv.at[c, edge + me], recv_sem.at[c]
            ).start()

    middle = SLAB_BLOCKS // 2
    owns_first = me < edge
    owns_last = me >= pieces - edge

    def send_middle(c):
        for v in range(groups):

            @pl.when(owns_first)
            def _(v=v):
                pltpu.make_async_remote_copy(
                    src_ref=send.at[c, middle * groups + v],
                    dst_ref=recv.at[c, edge + pieces + lax.rem(me, edge)],
                    send_sem=middle_sem.at[c],
                    recv_sem=halo_recv_sem.at[c, 1],
                    device_id={"space": (middle - 1) * groups + v},
                    device_id_type=MESH,
                ).start()

            @pl.when(owns_last)
            def _(v=v):
                pltpu.make_async_remote_copy(
                    src_ref=send.at[c, (middle - 1) * groups + v],
                    dst_ref=recv.at[c, lax.rem(me + edge - (pieces - edge) % edge, edge)],
                    send_sem=middle_sem.at[c],
                    recv_sem=halo_recv_sem.at[c, 0],
                    device_id={"space": middle * groups + v},
                    device_id_type=MESH,
                ).start()

    def send_chunk(c):
        @pl.loop(0, space)
        def _(d):
            send_piece(c, turn(me, d, space))

        send_middle(c)

    @pl.loop(0, space)
    def _(d):
        dest = lax.rem(me + d, space)

        @pl.when(dest != me)
        def _():
            pltpu.make_async_remote_copy(
                src_ref=cap_send.at[dest // groups],
                dst_ref=cap_recv.at[edge + me],
                send_sem=cap_send_sem,
                recv_sem=cap_recv_sem,
                device_id={"space": dest},
                device_id_type=MESH,
            ).start()

        @pl.when(dest == me)
        def _():
            pltpu.make_async_copy(
                cap_send.at[dest // groups], cap_recv.at[edge + me], cap_recv_sem
            ).start()

    def edges(buffer, send_sems, recv_sems):
        up = pltpu.make_async_remote_copy(
            src_ref=buffer.at[pl.ds(pieces, edge)],
            dst_ref=buffer.at[pl.ds(0, edge)],
            send_sem=send_sems.at[0],
            recv_sem=recv_sems.at[0],
            device_id={"space": lax.rem(me + groups, space)},
            device_id_type=MESH,
        )
        down = pltpu.make_async_remote_copy(
            src_ref=buffer.at[pl.ds(edge, edge)],
            dst_ref=buffer.at[pl.ds(edge + pieces, edge)],
            send_sem=send_sems.at[1],
            recv_sem=recv_sems.at[1],
            device_id={"space": lax.rem(me + space - groups, space)},
            device_id_type=MESH,
        )
        return up, down

    sends_up = {False: tile < SLAB_BLOCKS - 1}
    sends_up[True] = jnp.logical_and(sends_up[False], tile != middle - 1)
    sends_down = {False: tile > 0}
    sends_down[True] = jnp.logical_and(sends_down[False], tile != middle)

    def start_edges(*args, direct=False):
        up, down = edges(*args)

        @pl.when(sends_up[direct])
        def _():
            up.start()

        @pl.when(sends_down[direct])
        def _():
            down.start()

    def wait_edges(*args):
        up, down = edges(*args)

        @pl.when(tile > 0)
        def _():
            up.wait_recv()

        @pl.when(tile < SLAB_BLOCKS - 1)
        def _():
            down.wait_recv()

    def wait_edges_sent(*args, direct=False):
        up, down = edges(*args)

        @pl.when(sends_up[direct])
        def _():
            up.wait_send()

        @pl.when(sends_down[direct])
        def _():
            down.wait_send()

    cap_edges = (cap_recv, edge_send_sem, edge_recv_sem)

    @pl.loop(0, SLAB_BLOCKS)
    def _(i):
        t = turn(tile, i, SLAB_BLOCKS)
        slot = lax.rem(i, 2)

        @pl.when(i + 1 < SLAB_BLOCKS)
        def _():
            state_copy(i + 1).start()

        state_copy(i).wait()
        for j in range(rows_z):
            lanes = pl.ds(j * NY, NY)
            logs = jnp.dot(
                weights[...], states[slot, 0, :, lanes], preferred_element_type=jnp.float32
            )
            start = jnp.dot(
                weights[...], states[slot, 1, :, lanes], preferred_element_type=jnp.float32
            )
            live = live_ref[pl.ds(t, 1), lanes].astype(jnp.float32)
            perm = live * jnp.exp(logs.astype(jnp.bfloat16).astype(jnp.float32))
            for v in range(groups):
                for c in range(chunks):
                    r = v * share + c * CHUNK
                    both = jnp.concatenate([perm[r : r + CHUNK], start[r : r + CHUNK]], axis=0)
                    send[c, t * groups + v, :, lanes] = both.astype(jnp.bfloat16)

        @pl.loop(0, groups)
        def _(v):
            send_piece(0, t * groups + v)

        @pl.when(i == 2)
        def _():
            pltpu.make_async_copy(
                cap_recv.at[pl.ds(edge, pieces)], cap_recv.at[pl.ds(edge, pieces)], cap_recv_sem
            ).wait()
            start_edges(*cap_edges)

    send_middle(0)

    @pl.loop(1, min(depth, chunks))
    def _(c):
        send_chunk(c)

    source_rows[...] = jnp.zeros_like(source_rows)
    cell = lax.broadcasted_iota(jnp.int32, source_rows.shape, 0) * PLANE
    cell = cell + lax.broadcasted_iota(jnp.int32, source_rows.shape, 1)

    @pl.loop(0, wells)
    def _(w):
        for shift in (-1, 0, 1):
            t = jnp.clip(tile + shift, 0, SLAB_BLOCKS - 1)
            spot = where_ref[t, w] + (HALO + shift * TX) * PLANE
            rate = speed_ref[t, w] * (1.0 / 16.0)
            source_rows[...] += jnp.where(cell == spot, rate, 0.0)

    wait_edges(*cap_edges)

    for x in range(PADDED):
        for z in range(NZ):
            held = cap_recv[
                x * per_plane + z // rows_z, :, (z % rows_z) * NY : (z % rows_z + 1) * NY
            ]
            storage[x, z] = jnp.broadcast_to(held * (1.0 / 16.0), (CHUNK, NY))
            source[x, z] = jnp.broadcast_to(
                source_rows[x : x + 1, z * NY : (z + 1) * NY], (CHUNK, NY)
            )

    lane = lax.broadcasted_iota(jnp.int32, (CHUNK, NY), 1)
    first, last = lane == 0, lane == NY - 1

    def fields(c, x, z):
        both = recv[
            c, x * per_plane + z // rows_z, :, pl.ds((z % rows_z) * NY, NY)
        ].astype(jnp.float32)
        return both[:CHUNK], both[CHUNK:]

    def keep(b, x, z, p, perm):
        h = perm / (32.0 + 8.0 * p * p)
        press[b, x, z] = p
        flow[b, x, z] = h
        carried[b, x, z] = h * p

    def updated(b, x, z, start):
        p, h = press[b, x, z], flow[b, x, z]
        sides = [(x - 1, z), (x + 1, z)]
        if z > 0:
            sides.append((x, z - 1))
        if z < NZ - 1:
            sides.append((x, z + 1))
        p_left = jnp.where(first, 0.0, pltpu.roll(p, 1, 1))
        h_left = jnp.where(first, 0.0, pltpu.roll(h, 1, 1))
        p_right = jnp.where(last, 0.0, pltpu.roll(p, NY - 1, 1))
        h_right = jnp.where(last, 0.0, pltpu.roll(h, NY - 1, 1))
        p_sum = p_left + p_right
        h_sum = h_left + h_right
        hp_sum = h_left * p_left + h_right * p_right
        for at in sides:
            p_sum = p_sum + press[(b,) + at]
            h_sum = h_sum + flow[(b,) + at]
            hp_sum = hp_sum + carried[(b,) + at]
        s = storage[x, z]
        above = s * start + source[x, z] + h * p_sum + hp_sum
        below = s + 6.0 * h + h_sum
        return above / below

    def relax(c):
        @pl.loop(0, PADDED)
        def _(x):
            for z in range(NZ):
                perm, start = fields(c, x, z)
                keep(0, x, z, start, perm)

        for sweep in range(SWEEPS):
            b = sweep % 2
            reach = SWEEPS - 1 - sweep
            low = HALO - jnp.where(tile == 0, 0, reach)
            high = HALO + TX + jnp.where(tile == SLAB_BLOCKS - 1, 0, reach)

            def plane(x, _, b=b, sweep=sweep):
                for z in range(NZ):
                    perm, start = fields(c, x, z)
                    p = updated(b, x, z, start)
                    if sweep < SWEEPS - 1:
                        keep(1 - b, x, z, p, perm)
                    else:
                        result[c, x - HALO, z] = p
                return 0

            lax.fori_loop(low, high, plane, 0)

    def out_copy(c):
        return pltpu.make_async_copy(
            result.at[c], out_ref.at[:, :, pl.ds(c * CHUNK, CHUNK), :], out_sem.at[c]
        )

    def halo(c):
        return recv.at[c], halo_send_sem.at[c], halo_recv_sem.at[c]

    @pl.loop(0, chunks + 1)
    def _(c):
        @pl.when(c < chunks)
        def _():
            got = recv.at[c, pl.ds(edge, pieces)]
            pltpu.make_async_copy(got, got, recv_sem.at[c]).wait()
            start_edges(*halo(c), direct=True)

        @pl.when(c + depth < chunks)
        def _():
            send_chunk(c + depth)

        @pl.when(c > 0)
        def _():
            wait_edges(*halo(c - 1))
            relax(c - 1)
            out_copy(c - 1).start()

    @pl.loop(0, chunks)
    def _(c):
        sent = send.at[c, pl.ds(0, space - 1)]
        pltpu.make_async_copy(sent, sent, send_sem.at[c]).wait()
        wait_edges_sent(*halo(c), direct=True)
        sent_too = send.at[c, pl.ds(0, groups)]

        @pl.when(jnp.logical_or(owns_first, owns_last))
        def _():
            pltpu.make_async_copy(sent_too, sent_too, middle_sem.at[c]).wait()

        out_copy(c).wait()

    sent = cap_recv.at[pl.ds(0, space - 1)]
    pltpu.make_async_copy(sent, sent, cap_send_sem).wait()
    wait_edges_sent(*cap_edges)


def on_device(
    prior_states,
    mixing_matrix,
    capacity_factor,
    live_flags,
    borehole_block_location,
    borehole_injection_speed,
):
    space = lax.axis_size("space")
    groups = space // SLAB_BLOCKS
    members = mixing_matrix.shape[0]
    share = members // groups
    chunks = share // CHUNK
    piece = prior_states.shape[3]
    per_plane = PLANE // piece
    padded_pieces = PADDED * per_plane
    by_tile = prior_states.transpose(2, 0, 1, 3)
    vmem = pl.BlockSpec(memory_space=pltpu.VMEM)
    smem = pl.BlockSpec(memory_space=pltpu.SMEM)
    hbm = pl.BlockSpec(memory_space=pl.ANY)
    dma = pltpu.SemaphoreType.DMA
    slab = (PADDED, NZ, CHUNK, NY)
    out = pl.pallas_call(
        functools.partial(kernel, space, members, piece, 2),
        out_shape=jax.ShapeDtypeStruct((TX, NZ, share, NY), jnp.float32),
        in_specs=[hbm, vmem, vmem, vmem, smem, smem],
        out_specs=hbm,
        scratch_shapes=[
            pltpu.VMEM((members, members), jnp.bfloat16),
            pltpu.VMEM((2, 2, members, piece), jnp.bfloat16),
            pltpu.VMEM((chunks, space, 2 * CHUNK, piece), jnp.bfloat16),
            pltpu.VMEM((chunks, padded_pieces, 2 * CHUNK, piece), jnp.bfloat16),
            pltpu.VMEM((chunks, TX, NZ, CHUNK, NY), jnp.float32),
            pltpu.VMEM((2,) + slab, jnp.float32),
            pltpu.VMEM((2,) + slab, jnp.float32),
            pltpu.VMEM((2,) + slab, jnp.float32),
            pltpu.VMEM(slab, jnp.float32),
            pltpu.VMEM(slab, jnp.float32),
            pltpu.VMEM((-(-PADDED // 8) * 8, PLANE), jnp.float32),
            pltpu.VMEM((SLAB_BLOCKS, 1, piece), jnp.float32),
            pltpu.VMEM((padded_pieces, 1, piece), jnp.float32),
            dma((2,)),
            dma((chunks,)),
            dma((chunks,)),
            dma((chunks, 2)),
            dma((chunks, 2)),
            dma(()),
            dma(()),
            dma((2,)),
            dma((2,)),
            dma((chunks,)),
            dma((chunks,)),
        ],
        compiler_params=pltpu.CompilerParams(
            collective_id=0, has_side_effects=True, vmem_limit_bytes=56 * 1024 * 1024
        ),
    )(
        by_tile,
        mixing_matrix,
        capacity_factor,
        live_flags,
        borehole_block_location,
        borehole_injection_speed,
    )
    return out.transpose(2, 0, 1, 3)


def solution(mesh):
    placed = (
        P(None, None, None, ("groups", "space")),
        P(None, "groups"),
        P(None, ("groups", "space")),
        P(None, ("groups", "space")),
        P(None, "groups"),
        P(None, "groups"),
    )
    return jax.shard_map(
        on_device,
        mesh=mesh,
        in_specs=placed,
        out_specs=P(("groups", "space"), None, None, None),
        check_vma=False,
    )
```
